256 devices in a mesh: dp: 32 (over x, y, core), tp: 8 (over z).
Axes of the slice: x: 4, y: 4, z: 8, core: 2. Of those that a mesh axis runs over, the one named last changes fastest.
Arguments:
- queries: bfloat16 [1024, 24576], P('dp', 'tp')
- latent_cache: bfloat16 [1024, 256, 576], P('dp')
- fresh_latent_entry: bfloat16 [1024, 576], P('dp'), may hold values from -6 to 6
- lengths: int32 [1024], P('dp'), may hold values from 2 to 256, as said below
- key_up_matrix: bfloat16 [128, 128, 512], P('tp'), may hold values from -0.5 to 0.5
- value_up_matrix: bfloat16 [128, 512, 128], P('tp'), may hold values from -0.25 to 0.25
- out_proj: bfloat16 [16384, 7168], P('dp', 'tp'), may hold values from -0.09375 to 0.09375
- residual: bfloat16 [1024, 7168], P('dp', 'tp'), may hold values from -6 to 6
- norm_gain: bfloat16 [7168], P('tp'), may hold values from 0.099609375 to 1.8984375
- gate_weight: bfloat16 [7168, 18432], P('tp', 'dp'), may hold values from -0.0625 to 0.0625
- up_weight: bfloat16 [7168, 18432], P('tp', 'dp'), may hold values from -0.0625 to 0.0625
- down_weight: bfloat16 [18432, 7168], P('dp', 'tp'), may hold values from -0.09375 to 0.09375
Outputs:
- layer_out: bfloat16 [1024, 7168], P('dp', 'tp')
The draws below stay inside these ranges and needn't reach their ends.
Inputs may be any that keep to these rules, and one draw needn't show every extreme that they name: The used slots of a request are its first lengths[r]; some request uses all 256.
All inputs are finite; a program needn't handle non-finite values.
Results may differ from the reference program's by a relative error of at most 0.015.
Values may be sent and summed in bfloat16 or wider, within the bound.
A program may use at most 128 MiB of HBM per device.

```python
import jax
import jax.numpy as jnp
from jax import lax

D = 7168
FF = 18432
HEAD_TOTAL = 128
PLAIN_QUERY_DIM = 128
ROTARY_DIM = 64
LATENT_RANK = 512
VALUE_HEAD_DIM = 128
REQ_DEV = 32
CONTEXT_SLOTS = 256
REQUEST_TOTAL = 1024


def rope_keys(key):
    return jax.random.normal(key, (REQUEST_TOTAL, CONTEXT_SLOTS, ROTARY_DIM), jnp.float32)


def draw_latent_cache(key, part):
    rotated = rope_keys(key)
    key = jax.random.fold_in(key, 3)
    latent_rows = jax.random.normal(key, (REQUEST_TOTAL, CONTEXT_SLOTS, LATENT_RANK), jnp.float32)
    return jnp.concatenate([latent_rows, rotated], axis=2).astype(jnp.bfloat16)


def draw_queries(key, part):
    key = jax.random.fold_in(key, 4)
    base_query = jax.random.normal(key, (REQUEST_TOTAL, HEAD_TOTAL, PLAIN_QUERY_DIM + ROTARY_DIM), jnp.float32)
    return base_query.reshape(REQUEST_TOTAL, HEAD_TOTAL * (PLAIN_QUERY_DIM + ROTARY_DIM)).astype(jnp.bfloat16)


def draw_lengths(key, part):
    key = jax.random.fold_in(key, 8)
    group_count = REQUEST_TOTAL // REQ_DEV
    group_cap = jax.random.randint(jax.random.fold_in(key, 1), (group_count,), CONTEXT_SLOTS // 4, CONTEXT_SLOTS + 1)
    group_cap = jnp.repeat(group_cap, REQ_DEV)
    raw_bits = jax.random.randint(jax.random.fold_in(key, 2), (REQUEST_TOTAL,), 0, 1 << 20)
    used_slots = 2 + raw_bits % (group_cap - 1)
    longest = jax.random.randint(jax.random.fold_in(key, 3), (), 0, REQUEST_TOTAL)
    used_slots = used_slots.at[longest].set(CONTEXT_SLOTS)
    return used_slots.astype(jnp.int32)


def steps_of(key, shape, cuts, low, largest):
    def one(dim, blocks):
        heights = jax.random.uniform(jax.random.fold_in(jax.random.fold_in(key, 6), dim), (blocks,), jnp.float32, low / len(cuts), largest / len(cuts))
        return jnp.repeat(jnp.exp(heights), shape[dim] // blocks).reshape((-1,) + (1,) * (len(shape) - dim - 1))

    level = one(*cuts[0])
    for cut in cuts[1:]:
        level = level * one(*cut)
    return level


def centred(own_key, shape, width, bound, cuts=(), kind=jnp.bfloat16):
    result = width * jax.random.normal(own_key, shape, jnp.float32)
    if cuts:
        result = result * steps_of(own_key, shape, cuts, -0.22, 0.18)
    return jnp.clip(result, -bound, bound).astype(kind)


def setup_inputs(seed: int = 0) -> dict:
    keys = jax.random.split(jax.random.key(seed), 13)
    queries = draw_queries(jax.random.fold_in(keys[12], 71), 0)
    latent_cache = draw_latent_cache(jax.random.fold_in(keys[12], 71), 0)
    fresh_latent_entry = centred(keys[2], (REQUEST_TOTAL, LATENT_RANK + ROTARY_DIM), 1.0, 6.0, ((0, 32),))
    lengths = draw_lengths(jax.random.fold_in(keys[12], 71), 0)
    key_up_matrix = centred(keys[4], (HEAD_TOTAL, PLAIN_QUERY_DIM, LATENT_RANK), PLAIN_QUERY_DIM ** -0.5, 0.5, ((0, 8),))
    value_up_matrix = centred(keys[5], (HEAD_TOTAL, LATENT_RANK, VALUE_HEAD_DIM), LATENT_RANK ** -0.5, 0.25, ((0, 8),))
    out_proj = centred(keys[6], (HEAD_TOTAL * VALUE_HEAD_DIM, D), (HEAD_TOTAL * VALUE_HEAD_DIM // 4) ** -0.5, 0.09375, ((0, 32), (1, 8)))
    residual = centred(keys[7], (REQUEST_TOTAL, D), 1.0, 6.0, ((0, 32), (1, 8)))
    norm_gain = jnp.clip(1.0 + 0.18 * jax.random.normal(keys[8], (D,), jnp.float32), 0.099609375, 1.8984375).astype(jnp.bfloat16)
    gate_weight = centred(keys[9], (D, FF), D ** -0.5, 0.0625, ((0, 8), (1, 32)))
    up_weight = centred(keys[10], (D, FF), D ** -0.5, 0.0625, ((0, 8), (1, 32)))
    down_weight = centred(keys[11], (FF, D), (FF // 4) ** -0.5, 0.09375, ((0, 32), (1, 8)))
    return {"queries": queries, "latent_cache": latent_cache, "fresh_latent_entry": fresh_latent_entry, "lengths": lengths, "key_up_matrix": key_up_matrix, "value_up_matrix": value_up_matrix, "out_proj": out_proj, "residual": residual, "norm_gain": norm_gain, "gate_weight": gate_weight, "up_weight": up_weight, "down_weight": down_weight}


def attend(item):
    query_full, cache_rows, fresh_token_row, used = item
    score_scale = 1.0 / (PLAIN_QUERY_DIM + ROTARY_DIM) ** 0.5
    cache_float = cache_rows.astype(jnp.float32)
    scores = jnp.einsum('hc,jc->hj', query_full.astype(jnp.float32), cache_float) * score_scale
    new_score = jnp.einsum('hc,c->h', query_full.astype(jnp.float32), fresh_token_row.astype(jnp.float32)) * score_scale
    slot_used = (jnp.arange(CONTEXT_SLOTS, dtype=jnp.int32) < used)[None, :]
    masked = jnp.where(slot_used, scores, -1e+30)
    top_score = jnp.maximum(lax.optimization_barrier(jnp.max(masked, axis=1)), new_score)
    weights = jnp.where(slot_used, jnp.exp(masked - top_score[:, None]), 0.0)
    new_weight = jnp.exp(new_score - top_score)
    denom = lax.optimization_barrier(jnp.sum(weights, axis=1)) + new_weight
    slot_probabilities = (weights / denom[:, None]).astype(jnp.bfloat16)
    fresh_token_prob = (new_weight / denom).astype(jnp.bfloat16)
    latent_result = jnp.einsum('yk,kx->yx', slot_probabilities.astype(jnp.float32), cache_float[:, :LATENT_RANK])
    latent_result = latent_result + fresh_token_prob.astype(jnp.float32)[:, None] * fresh_token_row[None, :LATENT_RANK].astype(jnp.float32)
    return latent_result.astype(jnp.bfloat16)

def reference(queries, latent_cache, fresh_latent_entry, lengths, key_up_matrix, value_up_matrix, out_proj, residual, norm_gain, gate_weight, up_weight, down_weight):
    query_heads = queries.reshape(REQUEST_TOTAL, HEAD_TOTAL, PLAIN_QUERY_DIM + ROTARY_DIM)
    q_latent = jnp.einsum('rhk,hkl->rhl', query_heads[:, :, :PLAIN_QUERY_DIM].astype(jnp.float32), key_up_matrix.astype(jnp.float32)).astype(jnp.bfloat16)
    q_full = jnp.concatenate([q_latent, query_heads[:, :, PLAIN_QUERY_DIM:]], axis=2)
    attn_latent = lax.map(attend, (q_full, latent_cache, fresh_latent_entry, lengths.astype(jnp.int32)))
    attn_heads = jnp.einsum('rhl,hlv->rhv', attn_latent.astype(jnp.float32), value_up_matrix.astype(jnp.float32)).astype(jnp.bfloat16)
    attn_heads = attn_heads.reshape(REQUEST_TOTAL, HEAD_TOTAL * VALUE_HEAD_DIM)
    projected = jnp.dot(attn_heads, out_proj, preferred_element_type=jnp.float32)
    stream = (residual.astype(jnp.float32) + projected).astype(jnp.bfloat16)
    stream_f = stream.astype(jnp.float32)
    mean_square = lax.optimization_barrier(jnp.mean(stream_f * stream_f, axis=1, keepdims=True))
    normed = (stream_f * lax.rsqrt(mean_square + 1e-06) * norm_gain.astype(jnp.float32)).astype(jnp.bfloat16)
    gate_act = jnp.dot(normed, gate_weight, preferred_element_type=jnp.float32)
    up_act = jnp.dot(normed, up_weight, preferred_element_type=jnp.float32)
    hidden = (jax.nn.silu(gate_act) * up_act).astype(jnp.bfloat16)
    mlp_out = jnp.dot(hidden, down_weight, preferred_element_type=jnp.float32)
    return (stream_f + mlp_out).astype(jnp.bfloat16)
```

```python
import jax
import jax.numpy as jnp
from jax import lax
from jax.experimental import pallas as pl
from jax.experimental.pallas import tpu as pltpu
from jax.sharding import PartitionSpec as P

MESH = pl.DeviceIdType.MESH
BF = jnp.bfloat16
F32 = jnp.float32
D = 7168
EPS = 1e-06


def layer_kernel(
    attn, out_proj, residual, gain, gate, up, tails, down,
    out,
    wo, wg, wu, wt, wd, zbuf, ain, proj, rs1, sg, xn, st, stin, rcol, ownf, ownk, p4, z6, hid, dnb, rs2,
    w_l, w_s, w_r, z_s, z_r, a_s, a_r, p_s, p_r, g_s, g_r, t_s, t_r, z6_s, z6_r, h_s, h_r, d_s, d_r,
):
    dp = lax.axis_index("dp")
    k = lax.axis_index("tp")
    c = dp % 2
    p = dp // 2
    x = p // 4

    def chip(q):
        return (2 * q + c, k)

    def level(delta):
        return (dp, (k + 8 + delta) % 8)

    partner = (2 * p + 1 - c, k)

    def remote(src, dst, ssem, rsem, dev):
        return pltpu.make_async_remote_copy(
            src_ref=src, dst_ref=dst, send_sem=ssem, recv_sem=rsem, device_id=dev, device_id_type=MESH
        )

    def arrived(ref, sem):
        pltpu.make_async_copy(ref, ref, sem).wait()

    barrier = pltpu.get_barrier_semaphore()
    pl.semaphore_signal(barrier, inc=1, device_id=partner, device_id_type=MESH)

    def greet_plane(d, _):
        pl.semaphore_signal(barrier, inc=1, device_id=chip((p + d) % 16), device_id_type=MESH)
        return 0

    lax.fori_loop(1, 16, greet_plane, 0)

    def greet_level(d, _):
        pl.semaphore_signal(barrier, inc=1, device_id=level(d), device_id_type=MESH)
        return 0

    lax.fori_loop(1, 8, greet_level, 0)

    main = pl.ds(0, 512)
    d_main = pl.ds(pl.multiple_of(c * 512, 512), 512)
    d_tail = pl.ds(pl.multiple_of(1024 + c * 64, 64), 64)
    pairs = (
        (out_proj, wo.at[c]),
        (gate.at[:, main], wg.at[c]),
        (up.at[:, main], wu.at[c]),
        (tails, wt.at[c]),
        (down.at[main], wd.at[d_main]),
        (down.at[pl.ds(512, 64)], wd.at[d_tail]),
    )
    other_main = pl.ds(pl.multiple_of((1 - c) * 512, 512), 512)
    other_tail = pl.ds(pl.multiple_of(1024 + (1 - c) * 64, 64), 64)
    theirs = (wo.at[1 - c], wg.at[1 - c], wu.at[1 - c], wt.at[1 - c], wd.at[other_main], wd.at[other_tail])
    for n, (src, dst) in enumerate(pairs):
        pltpu.make_async_copy(src, dst, w_l.at[n]).start()

    pl.semaphore_wait(barrier, 23)

    dirs = (1, -1)

    def to_rows(blk, b, ref):
        q = 2 * blk + b

        @pl.when(q != p)
        def _():
            remote(ref, ain.at[p], a_s.at[q], a_r.at[p], chip(q)).start()

        @pl.when(q == p)
        def _():
            pltpu.make_async_copy(ref, ain.at[p], a_r.at[p]).start()

    for b in range(2):
        for di, d in enumerate(dirs):
            remote(attn.at[b], zbuf.at[k, b], z_s.at[di, 0, b], z_r.at[di, 0, b], level(d)).start()
    for n, (src, dst) in enumerate(pairs):
        remote(src, dst, w_s.at[n], w_r.at[n], partner).start()
    for b in range(2):
        to_rows(k, b, attn.at[b])
    for t in range(1, 5):
        for b in range(2):
            for di, d in enumerate(dirs):
                if t == 4 and b != di:
                    continue
                blk = (k + 8 - d * t) % 8
                ref = zbuf.at[blk, b]
                arrived(ref, z_r.at[di, t - 1, b])
                if t < 3 or (t == 3 and b == di):
                    remote(ref, ref, z_s.at[di, t, b], z_r.at[di, t, b], level(d)).start()
                to_rows(blk, b, ref)

    pltpu.make_async_copy(pairs[0][0], pairs[0][1], w_l.at[0]).wait()
    arrived(theirs[0], w_r.at[0])

    def project(g, _):
        first = ((x + 1 + g) % 4) * 4
        for y in range(4):
            arrived(ain.at[first + y], a_r.at[first + y])
        rows = ain[pl.ds(first, 4)].reshape(128, 1024)
        part = jnp.dot(rows, wo[...].reshape(1024, 896), preferred_element_type=F32)
        proj[pl.ds(first, 4)] = part.astype(BF).reshape(4, 32, 896)
        for y in range(4):
            q = first + y

            @pl.when(q != p)
            def _():
                remote(proj.at[q], rs1.at[p], p_s.at[q], p_r.at[p], chip(q)).start()

        return 0

    lax.fori_loop(0, 4, project, 0)

    def add_proj(d, acc):
        q = (p + d) % 16
        arrived(rs1.at[q], p_r.at[q])
        return acc + rs1[q].astype(F32)

    total = residual[...].astype(F32) + proj[p].astype(F32)
    total = lax.fori_loop(1, 16, add_proj, total)
    sg[p] = total.astype(BF)

    def spread(d, _):
        q = (p + d) % 16
        remote(sg.at[p], sg.at[p], g_s.at[q], g_r.at[p], chip(q)).start()
        return 0

    lax.fori_loop(1, 16, spread, 0)

    z6[0, 0, 1] = jnp.zeros((64, 1152), BF)
    z6[1, 0, 0] = jnp.zeros((64, 1152), BF)
    for n in range(1, 6):
        pltpu.make_async_copy(pairs[n][0], pairs[n][1], w_l.at[n]).wait()
        arrived(theirs[n], w_r.at[n])

    def gathered(d, _):
        q = (p + d) % 16
        arrived(sg.at[q], g_r.at[q])
        return 0

    lax.fori_loop(1, 16, gathered, 0)

    gain_f = gain[...].astype(F32)

    def scale(q, _):
        s = sg[pl.ds(4 * q, 4)].reshape(128, 896).astype(F32)
        xn[pl.ds(4 * q, 4)] = (s * gain_f).astype(BF).reshape(4, 32, 896)
        st[q] = lax.dot_general(
            jnp.ones((8, 896), F32),
            s * s,
            (((1,), (1,)), ((), ())),
            precision=lax.Precision.HIGHEST,
            preferred_element_type=F32,
        )
        return 0

    lax.fori_loop(0, 4, scale, 0)

    f = p // 2
    kk = (k + f) % 8

    def send_stat(d, _):
        lab = (kk + d) % 8
        remote(st.at[lab // 2], stin.at[d], t_s.at[d], t_r.at[d], level(d)).start()
        return 0

    lax.fori_loop(1, 8, send_stat, 0)

    def chain(t, _):
        lab_a = (kk + 4 - t + 8) % 8
        lab_b = jnp.where(t == 0, kk, (kk + 4 + t) % 8)
        rows = jnp.concatenate(
            [xn[pl.ds(2 * lab_a, 2)].reshape(64, 896), xn[pl.ds(2 * lab_b, 2)].reshape(64, 896)], axis=0
        )
        for h, w in enumerate((wg, wu)):
            for b in range(2):
                res = jnp.dot(rows, w[b], preferred_element_type=F32)
                ownf[0, h, :, b * 512 : b * 512 + 512] = res[:64]
                ownf[1, h, :, b * 512 : b * 512 + 512] = res[64:]
            res = jnp.dot(rows, wt[h], preferred_element_type=F32)
            ownf[0, h, :, 1024:] = res[:64]
            ownf[1, h, :, 1024:] = res[64:]

        @pl.when(t == 0)
        def _():
            p4[...] = ownf[0].astype(BF)
            for di, d in enumerate(dirs):
                remote(p4.at[di], z6.at[di, 0, di], z6_s.at[di, 0, di], z6_r.at[di, 0, di], level(d)).start()
            ownk[...] = ownf[1]

        @pl.when(t > 0)
        def _():
            for h in range(2):
                for di, d in enumerate(dirs):
                    ref = z6.at[di, t - 1, h]
                    if h == di:
                        arrived(ref, z6_r.at[di, t - 1, h])
                    else:

                        @pl.when(t > 1)
                        def _():
                            arrived(ref, z6_r.at[di, t - 1, h])

                    z6[di, t - 1, h] = (z6[di, t - 1, h].astype(F32) + ownf[di, h]).astype(BF)
                    remote(ref, z6.at[di, t, h], z6_s.at[di, t, h], z6_r.at[di, t, h], level(d)).start()

        return 0

    lax.fori_loop(0, 4, chain, 0)

    def add_stat(d, acc):
        arrived(stin.at[d], t_r.at[d])
        return acc + stin[d]

    square = lax.fori_loop(1, 8, add_stat, st[kk // 2])
    inv = lax.rsqrt(square / D + EPS)
    rcol[...] = jnp.transpose(jnp.broadcast_to(inv[0:1, :], (128, 128)))
    r = rcol[pl.ds(pl.multiple_of((kk % 2) * 64, 64), 64), :][:, 0:1]

    sums = []
    for h in range(2):
        for di in range(2):
            arrived(z6.at[di, 3, h], z6_r.at[di, 3, h])
        sums.append((ownk[h] + z6[0, 3, h].astype(F32) + z6[1, 3, h].astype(F32)) * r)

    def glu(g, u):
        return (g / (1.0 + jnp.exp(-g)) * u).astype(BF)

    t0, t1 = sums[0][:, 1024:], sums[1][:, 1024:]
    low = lax.broadcasted_iota(jnp.int32, (64, 128), 1) < 64
    t0r, t1r = pltpu.roll(t0, 64, 1), pltpu.roll(t1, 64, 1)
    hid[kk, :, :, 0:1024] = glu(sums[0][:, :1024], sums[1][:, :1024]).reshape(2, 32, 1024)
    hid[kk, :, :, 1024:] = glu(jnp.where(low, t0, t1r), jnp.where(low, t0r, t1)).reshape(2, 32, 128)

    for di, d in enumerate(dirs):
        for b in range(2):
            remote(hid.at[kk, b], hid.at[kk, b], h_s.at[di, 0, b], h_r.at[di, 0, b], level(d)).start()

    def lower(labs):
        n = 64 * len(labs)
        rows = [hid[lab].reshape(64, 1152) for lab in labs]
        rows = rows[0] if len(labs) == 1 else jnp.concatenate(rows, axis=0)
        part = jnp.dot(rows, wd[...], preferred_element_type=F32).astype(BF)
        for i, lab in enumerate(labs):
            dnb[pl.ds(2 * lab, 2)] = part[64 * i : 64 * i + 64].reshape(2, 32, 896)
            for b in range(2):
                q = 2 * lab + b

                @pl.when(q != p)
                def _():
                    remote(dnb.at[q], rs2.at[p], d_s.at[q], d_r.at[p], chip(q)).start()

    lower([kk])
    for t in range(1, 5):
        for b in range(2):
            for di, d in enumerate(dirs):
                if t == 4 and b != di:
                    continue
                ref = hid.at[(kk + 8 - d * t) % 8, b]
                arrived(ref, h_r.at[di, t - 1, b])
                if t < 3 or (t == 3 and b == di):
                    remote(ref, ref, h_s.at[di, t, b], h_r.at[di, t, b], level(d)).start()
        if t < 4:
            lower([(kk + 8 - t) % 8, (kk + t) % 8])
        else:
            lower([(kk + 4) % 8])

    def add_down(d, acc):
        q = (p + d) % 16
        arrived(rs2.at[q], d_r.at[q])
        return acc + rs2[q].astype(F32)

    total = sg[p].astype(F32) + dnb[p].astype(F32)
    total = lax.fori_loop(1, 16, add_down, total)
    out[...] = total.astype(BF)

    def sent(ref, sem):
        pltpu.make_async_copy(ref, ref, sem).wait()

    for n in range(6):
        sent(pairs[n][1], w_s.at[n])
    for di in range(2):
        for t in range(4):
            for b in range(2):
                if t < 3 or b == di:
                    sent(zbuf.at[0, 0], z_s.at[di, t, b])
                    sent(hid.at[0, 0], h_s.at[di, t, b])
                if t > 0 or b == di:
                    sent(z6.at[di, 0, 0], z6_s.at[di, t, b])

    def sent_plane(d, _):
        q = (p + d) % 16
        sent(ain.at[q], a_s.at[q])
        sent(proj.at[q], p_s.at[q])
        sent(sg.at[q], g_s.at[q])
        sent(dnb.at[q], d_s.at[q])
        return 0

    lax.fori_loop(1, 16, sent_plane, 0)

    def sent_stat(d, _):
        sent(stin.at[d], t_s.at[d])
        return 0

    lax.fori_loop(1, 8, sent_stat, 0)


def layer(attn, out_proj, residual, gain, gate, up, tails, down):
    vm = pl.BlockSpec(memory_space=pltpu.VMEM)
    hbm = pl.BlockSpec(memory_space=pl.ANY)
    dma = pltpu.SemaphoreType.DMA
    return pl.pallas_call(
        layer_kernel,
        out_shape=jax.ShapeDtypeStruct((32, 896), BF),
        in_specs=[vm, hbm, vm, vm, hbm, hbm, hbm, hbm],
        out_specs=vm,
        scratch_shapes=[
            pltpu.VMEM((2, 512, 896), BF),
            pltpu.VMEM((2, 896, 512), BF),
            pltpu.VMEM((2, 896, 512), BF),
            pltpu.VMEM((2, 896, 128), BF),
            pltpu.VMEM((1152, 896), BF),
            pltpu.VMEM((8, 2, 32, 1024), BF),
            pltpu.VMEM((16, 32, 1024), BF),
            pltpu.VMEM((16, 32, 896), BF),
            pltpu.VMEM((16, 32, 896), BF),
            pltpu.VMEM((16, 32, 896), BF),
            pltpu.VMEM((16, 32, 896), BF),
            pltpu.VMEM((4, 8, 128), F32),
            pltpu.VMEM((8, 8, 128), F32),
            pltpu.VMEM((128, 128), F32),
            pltpu.VMEM((2, 2, 64, 1152), F32),
            pltpu.VMEM((2, 64, 1152), F32),
            pltpu.VMEM((2, 64, 1152), BF),
            pltpu.VMEM((2, 4, 2, 64, 1152), BF),
            pltpu.VMEM((8, 2, 32, 1152), BF),
            pltpu.VMEM((16, 32, 896), BF),
            pltpu.VMEM((16, 32, 896), BF),
            dma((6,)), dma((6,)), dma((6,)),
            dma((2, 4, 2)), dma((2, 4, 2)),
            dma((16,)), dma((16,)),
            dma((16,)), dma((16,)),
            dma((16,)), dma((16,)),
            dma((8,)), dma((8,)),
            dma((2, 4, 2)), dma((2, 4, 2)),
            dma((2, 4, 2)), dma((2, 4, 2)),
            dma((16,)), dma((16,)),
        ],
        compiler_params=pltpu.CompilerParams(
            collective_id=0, has_side_effects=True, vmem_limit_bytes=48 * 2**20
        ),
        name="layer",
    )(attn, out_proj, residual, gain, gate, up, tails, down)


def attention(queries, latent_cache, fresh_latent_entry, lengths, key_up_matrix, value_up_matrix):
    own_rows = queries.shape[0]
    head_count, nope_width, latent_width = key_up_matrix.shape
    rope_width = latent_cache.shape[2] - latent_width
    slot_count = latent_cache.shape[1]
    score_scale = 1.0 / (nope_width + rope_width) ** 0.5
    query_heads = queries.reshape(own_rows, head_count, nope_width + rope_width)
    q_latent = jnp.einsum(
        "rhk,hkl->rhl",
        query_heads[:, :, :nope_width],
        key_up_matrix,
        preferred_element_type=jnp.float32,
    ).astype(jnp.bfloat16)
    q_full = jnp.concatenate([q_latent, query_heads[:, :, nope_width:]], axis=2)
    scores = (
        jnp.einsum("rhc,rjc->rhj", q_full, latent_cache, preferred_element_type=jnp.float32)
        * score_scale
    )
    new_score = (
        jnp.einsum("rhc,rc->rh", q_full, fresh_latent_entry, preferred_element_type=jnp.float32)
        * score_scale
    )
    slot_used = (lax.broadcasted_iota(jnp.int32, (own_rows, slot_count), 1) < lengths[:, None])[
        :, None, :
    ]
    masked = jnp.where(slot_used, scores, -1e30)
    top_score = jnp.maximum(jnp.max(masked, axis=2), new_score)
    weights = jnp.where(slot_used, jnp.exp(masked - top_score[:, :, None]), 0.0)
    new_weight = jnp.exp(new_score - top_score)
    denom = jnp.sum(weights, axis=2) + new_weight
    slot_probabilities = (weights / denom[:, :, None]).astype(jnp.bfloat16)
    fresh_token_prob = (new_weight / denom).astype(jnp.bfloat16)
    latent_result = jnp.einsum(
        "rhj,rjl->rhl",
        slot_probabilities,
        latent_cache[:, :, :latent_width],
        preferred_element_type=jnp.float32,
    )
    latent_result = latent_result + fresh_token_prob.astype(jnp.float32)[
        :, :, None
    ] * fresh_latent_entry[:, None, :latent_width].astype(jnp.float32)
    attn_latent = latent_result.astype(jnp.bfloat16)
    return jnp.einsum(
        "rhl,hlv->rhv", attn_latent, value_up_matrix, preferred_element_type=jnp.float32
    ).astype(jnp.bfloat16)


def body(
    queries,
    latent_cache,
    fresh_latent_entry,
    lengths,
    key_up_matrix,
    value_up_matrix,
    out_proj,
    residual,
    norm_gain,
    gate_weight,
    up_weight,
    down_weight,
):
    tails = jnp.concatenate([gate_weight[:, 512:], up_weight[:, 512:]], axis=1)
    heads = attention(
        queries, latent_cache, fresh_latent_entry, lengths, key_up_matrix, value_up_matrix
    )
    attn = heads.reshape(32, 2, 1024).transpose(1, 0, 2)
    return layer(
        attn, out_proj, residual, norm_gain.reshape(1, -1), gate_weight, up_weight, tails, down_weight
    )


def solution(mesh):
    return jax.shard_map(
        body,
        mesh=mesh,
        in_specs=(
            P("dp", "tp"),
            P("dp", None, None),
            P("dp", None),
            P("dp"),
            P("tp", None, None),
            P("tp", None, None),
            P("dp", "tp"),
            P("dp", "tp"),
            P("tp"),
            P("tp", "dp"),
            P("tp", "dp"),
            P("dp", "tp"),
        ),
        out_specs=P("dp", "tp"),
        check_vma=False,
    )
```

```python
import jax
import jax.numpy as jnp
from jax import lax
from jax.experimental import pallas as pl
from jax.experimental.pallas import tpu as pltpu
from jax.sharding import PartitionSpec as P

MESH = pl.DeviceIdType.MESH
BF = jnp.bfloat16
F32 = jnp.float32
D = 7168
EPS = 1e-06
GROUP = 8
GROUPS = 4
SCALE = 1.0 / 192**0.5


def layer_kernel(
    lengths, q_full, fresh, cache, value_up, out_proj, residual, gain, gate, up, down,
    out,
    keys, vup, fresh_f, lat, attn, wo, wg, wu, wd, zbuf, ain, proj, rs1, sg, xn, st, stin, rcol, own, p4, z6, hid, dnb, rs2,
    c_s, v_s, w_l, w_s, w_r, z_s, z_r, a_s, a_r, p_s, p_r, g_s, g_r, t_s, t_r, z6_s, z6_r, h_s, h_r, d_s, d_r,
):
    dp = lax.axis_index("dp")
    k = lax.axis_index("tp")
    c = dp % 2
    p = dp // 2

    def chip(q):
        return (2 * q + c, k)

    def level(delta):
        return (dp, (k + 8 + delta) % 8)

    partner = (2 * p + 1 - c, k)
    dirs = (1, -1)
    leaving = []

    def remote(src, dst, ssem, rsem, dev):
        return pltpu.make_async_remote_copy(
            src_ref=src, dst_ref=dst, send_sem=ssem, recv_sem=rsem, device_id=dev, device_id_type=MESH
        )

    def send(src, dst, ssem, rsem, dev):
        remote(src, dst, ssem, rsem, dev).start()
        leaving.append((src, ssem))

    def arrived(ref, sem):
        pltpu.make_async_copy(ref, ref, sem).wait()

    barrier = pltpu.get_barrier_semaphore()
    pl.semaphore_signal(barrier, inc=1, device_id=partner, device_id_type=MESH)

    def greet_plane(d, _):
        pl.semaphore_signal(barrier, inc=1, device_id=chip((p + d) % 16), device_id_type=MESH)
        return 0

    lax.fori_loop(1, 16, greet_plane, 0)

    def greet_level(d, _):
        pl.semaphore_signal(barrier, inc=1, device_id=level(d), device_id_type=MESH)
        return 0

    lax.fori_loop(1, 8, greet_level, 0)

    for g in range(GROUPS):
        rows = pl.ds(g * GROUP, GROUP)
        pltpu.make_async_copy(cache.at[rows], keys.at[rows], c_s.at[g]).start()
        if g == 1:
            pltpu.make_async_copy(value_up, vup, v_s).start()
    pairs = ((out_proj, wo.at[c]), (gate, wg.at[c]), (up, wu.at[c]), (down, wd.at[c]))
    theirs = (wo.at[1 - c], wg.at[1 - c], wu.at[1 - c], wd.at[1 - c])
    for n, (src, dst) in enumerate(pairs):
        pltpu.make_async_copy(src, dst, w_l.at[n]).start()
    fresh_f[...] = fresh[...].astype(F32)

    def weight(n):
        pltpu.make_async_copy(pairs[n][0], pairs[n][1], w_l.at[n]).wait()
        arrived(theirs[n], w_r.at[n])

    slot = lax.broadcasted_iota(jnp.int32, (16, 256), 1)

    def attend(g):
        arrived(keys.at[pl.ds(g * GROUP, GROUP)], c_s.at[g])
        scores, new_score, used = [], [], []
        for i in range(GROUP):
            r = g * GROUP + i
            q = q_full[r]
            entry = fresh_f[pl.ds(r, 1), :]
            scores.append(jnp.dot(q, keys[r], preferred_element_type=F32) * SCALE)
            new_score.append(jnp.sum(q.astype(F32) * entry, axis=1, keepdims=True) * SCALE)
            used.append(slot < lengths[r])
        masked = jnp.concatenate([jnp.where(u, v, -1e30) for u, v in zip(used, scores)], axis=0)
        new_score = jnp.concatenate(new_score, axis=0)
        top = jnp.maximum(jnp.max(masked, axis=1, keepdims=True), new_score)
        powers = jnp.exp(masked - top)
        weights = jnp.concatenate(
            [jnp.where(u, powers[16 * i : 16 * i + 16], 0.0) for i, u in enumerate(used)], axis=0
        )
        new_weight = jnp.exp(new_score - top)
        denom = jnp.sum(weights, axis=1, keepdims=True) + new_weight
        probs = (weights / denom).astype(BF)
        new_prob = (new_weight / denom).astype(BF).astype(F32)
        for i in range(GROUP):
            r = g * GROUP + i
            own_rows = slice(16 * i, 16 * i + 16)
            res = lax.dot_general(
                probs[own_rows], keys[r, 0:512, :], (((1,), (1,)), ((), ())), preferred_element_type=F32
            )
            lat[:, r % 16, :] = res + new_prob[own_rows] * fresh_f[pl.ds(r, 1), 0:512]

    def attend_groups(first, last):
        lax.fori_loop(first, last, lambda g, _: (attend(g), 0)[1], 0)

    def heads_out(ch):
        def head(h, _):
            res = jnp.dot(lat[h].astype(BF), vup[h], preferred_element_type=F32)
            attn[h // 8, ch, :, pl.ds(pl.multiple_of((h % 8) * 128, 128), 128)] = res.astype(BF)
            return 0

        lax.fori_loop(0, 16, head, 0, unroll=4)

    def to_rows(blk, b, ch, ref):
        q = 2 * blk + b

        @pl.when(q != p)
        def _():
            remote(ref, ain.at[ch, p], a_s.at[ch, q], a_r.at[ch, p], chip(q)).start()

        @pl.when(q == p)
        def _():
            pltpu.make_async_copy(ref, ain.at[ch, p], a_r.at[ch, p]).start()

    def heads_start(ch):
        for b in range(2):
            for di, d in enumerate(dirs):
                send(attn.at[b, ch], zbuf.at[k, b, ch], z_s.at[ch, di, 0, b], z_r.at[ch, di, 0, b], level(d))
        for b in range(2):
            to_rows(k, b, ch, attn.at[b, ch])

    def heads_step(ch, t):
        for b in range(2):
            for di, d in enumerate(dirs):
                if t == 4 and b != di:
                    continue
                blk = (k + 8 - d * t) % 8
                ref = zbuf.at[blk, b, ch]
                arrived(ref, z_r.at[ch, di, t - 1, b])
                if t < 3 or (t == 3 and b == di):
                    send(ref, ref, z_s.at[ch, di, t, b], z_r.at[ch, di, t, b], level(d))
                to_rows(blk, b, ch, ref)

    def swap():
        pl.semaphore_wait(barrier, 23)
        for n, (src, dst) in enumerate(pairs):
            send(src, dst, w_s.at[n], w_r.at[n], partner)

    def project(ch, send_now):
        def group(g, _):
            first = (((p // 8) + 1 + g) % 2) * 8

            def wait_rows(j, _):
                arrived(ain.at[ch, first + j], a_r.at[ch, first + j])
                return 0

            lax.fori_loop(0, 8, wait_rows, 0)
            rows = ain[ch, pl.ds(first, 8)].reshape(128, 1024)
            part = jnp.dot(rows, wo[...].reshape(1024, 896), preferred_element_type=F32)
            proj[ch, pl.ds(first, 8)] = part.astype(BF).reshape(8, 16, 896)
            if send_now:
                for j in range(8):

                    @pl.when(first + j != p)
                    def _():
                        q = first + j
                        remote(proj.at[ch, q], rs1.at[ch, p], p_s.at[ch, q], p_r.at[ch, p], chip(q)).start()

            return 0

        lax.fori_loop(0, 2, group, 0)

    def send_proj(ch):
        def one(d, _):
            q = (p + d) % 16
            remote(proj.at[ch, q], rs1.at[ch, p], p_s.at[ch, q], p_r.at[ch, p], chip(q)).start()
            return 0

        lax.fori_loop(1, 16, one, 0)

    def join(ch):
        def add(d, acc):
            q = (p + d) % 16
            arrived(rs1.at[ch, q], p_r.at[ch, q])
            return acc + rs1[ch, q].astype(F32)

        total = residual[16 * ch : 16 * ch + 16].astype(F32) + proj[ch, p].astype(F32)
        sg[ch, p] = lax.fori_loop(1, 16, add, total).astype(BF)

        def spread(d, _):
            q = (p + d) % 16
            remote(sg.at[ch, p], sg.at[ch, p], g_s.at[ch, q], g_r.at[ch, p], chip(q)).start()
            return 0

        lax.fori_loop(1, 16, spread, 0)

    f = p // 2
    kk = (k + f) % 8

    def lab(delta):
        return (kk + 8 + delta) % 8

    def expand(ch):
        def gathered(d, _):
            q = (p + d) % 16
            arrived(sg.at[ch, q], g_r.at[ch, q])
            return 0

        lax.fori_loop(1, 16, gathered, 0)
        gain_f = gain[...].astype(F32)

        def scale(g, _):
            s = sg[ch, pl.ds(8 * g, 8)].reshape(128, 896).astype(F32)
            xn[ch, pl.ds(8 * g, 8)] = (s * gain_f).astype(BF).reshape(8, 16, 896)
            sq = s * s
            lanes = sq[:, 0:128]
            for i in range(1, 7):
                lanes = lanes + sq[:, 128 * i : 128 * i + 128]
            st[ch, g] = jnp.broadcast_to(jnp.sum(jnp.transpose(lanes), axis=0, keepdims=True), (8, 128))
            return 0

        lax.fori_loop(0, 2, scale, 0)
        rows = xn[ch].reshape(256, 896)
        for h, w in enumerate((wg, wu)):
            res = lax.dot_general(
                rows, w[...].reshape(1152, 896), (((1,), (1,)), ((), ())), preferred_element_type=F32
            )
            own[ch, h] = res.reshape(8, 32, 1152)
            p4[ch, h] = own[ch, h, lab(4)].astype(BF)
            send(
                p4.at[ch, h], z6.at[ch, h, 0, h], z6_s.at[ch, h, 0, h], z6_r.at[ch, h, 0, h], level(dirs[h])
            )

        def send_stat(d, _):
            remote(
                st.at[ch, lab(d) // 4], stin.at[ch, d], t_s.at[ch, d], t_r.at[ch, d], level(d)
            ).start()
            return 0

        lax.fori_loop(1, 8, send_stat, 0)

    def chain(ch, t):
        for h in range(2):
            for di, d in enumerate(dirs):
                ref = z6.at[ch, di, t - 1, h]
                mine = own[ch, h, lab(d * (4 - t))]
                if h == di or t > 1:
                    arrived(ref, z6_r.at[ch, di, t - 1, h])
                    mine = mine + z6[ch, di, t - 1, h].astype(F32)
                z6[ch, di, t - 1, h] = mine.astype(BF)
                send(ref, z6.at[ch, di, t, h], z6_s.at[ch, di, t, h], z6_r.at[ch, di, t, h], level(d))

    def lower(ch, labs):
        n = 32 * len(labs)
        rows = [hid[ch, l].reshape(32, 1152) for l in labs]
        rows = rows[0] if len(labs) == 1 else jnp.concatenate(rows, axis=0)
        part = jnp.dot(rows, wd[...].reshape(1152, 896), preferred_element_type=F32).astype(BF)
        for i, l in enumerate(labs):
            dnb[ch, pl.ds(2 * l, 2)] = part[32 * i : 32 * i + 32].reshape(2, 16, 896)
            for b in range(2):
                q = 2 * l + b

                @pl.when(q != p)
                def _():
                    remote(dnb.at[ch, q], rs2.at[ch, p], d_s.at[ch, q], d_r.at[ch, p], chip(q)).start()

    def activate(ch):
        def add_stat(d, acc):
            arrived(stin.at[ch, d], t_r.at[ch, d])
            return acc + stin[ch, d]

        square = lax.fori_loop(1, 8, add_stat, st[ch, kk // 4])
        inv = lax.rsqrt(square / D + EPS)
        rcol[ch] = jnp.transpose(jnp.broadcast_to(inv[0:1, :], (128, 128)))
        r = rcol[ch, pl.ds(pl.multiple_of((kk % 4) * 32, 32), 32), :][:, 0:1]
        sums = []
        for h in range(2):
            for di in range(2):
                arrived(z6.at[ch, di, 3, h], z6_r.at[ch, di, 3, h])
            total = own[ch, h, kk] + z6[ch, 0, 3, h].astype(F32) + z6[ch, 1, 3, h].astype(F32)
            sums.append(total * r)
        units = sums[0] / (1.0 + jnp.exp(-sums[0])) * sums[1]
        hid[ch, kk] = units.astype(BF).reshape(2, 16, 1152)
        for di, d in enumerate(dirs):
            for b in range(2):
                ref = hid.at[ch, kk, b]
                send(ref, ref, h_s.at[ch, di, 0, b], h_r.at[ch, di, 0, b], level(d))

    def collect(ch, t):
        for b in range(2):
            for di, d in enumerate(dirs):
                if t == 4 and b != di:
                    continue
                ref = hid.at[ch, lab(-d * t), b]
                arrived(ref, h_r.at[ch, di, t - 1, b])
                if t < 3 or (t == 3 and b == di):
                    send(ref, ref, h_s.at[ch, di, t, b], h_r.at[ch, di, t, b], level(d))

    def finish(ch):
        def add(d, acc):
            q = (p + d) % 16
            arrived(rs2.at[ch, q], d_r.at[ch, q])
            return acc + rs2[ch, q].astype(F32)

        total = sg[ch, p].astype(F32) + dnb[ch, p].astype(F32)
        out[16 * ch : 16 * ch + 16] = lax.fori_loop(1, 16, add, total).astype(BF)

    attend_groups(0, 1)
    swap()
    attend_groups(1, 2)
    pltpu.make_async_copy(value_up, vup, v_s).wait()
    heads_out(0)
    heads_start(0)
    attend_groups(2, 3)
    heads_step(0, 1)
    attend_groups(3, 4)
    heads_step(0, 2)
    heads_out(1)
    heads_start(1)
    heads_step(0, 3)
    heads_step(1, 1)
    heads_step(0, 4)
    heads_step(1, 2)
    weight(0)
    heads_step(1, 3)
    project(0, True)
    heads_step(1, 4)
    project(1, False)
    join(0)
    send_proj(1)
    weight(1)
    weight(2)
    expand(0)
    chain(0, 1)
    join(1)
    chain(0, 2)
    chain(0, 3)
    expand(1)
    chain(1, 1)
    activate(0)
    chain(1, 2)
    weight(3)
    collect(0, 1)
    lower(0, [kk])
    chain(1, 3)
    collect(0, 2)
    lower(0, [lab(1), lab(-1)])
    activate(1)
    collect(0, 3)
    lower(0, [lab(2), lab(-2)])
    collect(1, 1)
    lower(1, [kk])
    collect(0, 4)
    lower(0, [lab(3), lab(-3)])
    collect(1, 2)
    lower(0, [lab(4)])
    lower(1, [lab(1), lab(-1)])
    collect(1, 3)
    lower(1, [lab(2), lab(-2)])
    collect(1, 4)
    lower(1, [lab(3), lab(-3)])
    lower(1, [lab(4)])
    finish(0)
    finish(1)

    for ref, sem in leaving:
        pltpu.make_async_copy(ref, ref, sem).wait()

    def sent_plane(d, _):
        q = (p + d) % 16
        for ch in range(2):
            for ref, sem in ((ain, a_s), (proj, p_s), (sg, g_s), (dnb, d_s)):
                pltpu.make_async_copy(ref.at[ch, q], ref.at[ch, q], sem.at[ch, q]).wait()
        return 0

    lax.fori_loop(1, 16, sent_plane, 0)

    def sent_stat(d, _):
        for ch in range(2):
            pltpu.make_async_copy(stin.at[ch, d], stin.at[ch, d], t_s.at[ch, d]).wait()
        return 0

    lax.fori_loop(1, 8, sent_stat, 0)


def layer(lengths, q_full, fresh, cache, value_up, out_proj, residual, gain, gate, up, down):
    vm = pl.BlockSpec(memory_space=pltpu.VMEM)
    hbm = pl.BlockSpec(memory_space=pl.ANY)
    dma = pltpu.SemaphoreType.DMA
    plane = pltpu.VMEM((2, 16, 16, 896), BF)
    return pl.pallas_call(
        layer_kernel,
        out_shape=jax.ShapeDtypeStruct((32, 896), BF),
        in_specs=[pl.BlockSpec(memory_space=pltpu.SMEM), vm, vm, hbm, hbm, hbm, vm, vm, hbm, hbm, hbm],
        out_specs=vm,
        scratch_shapes=[
            pltpu.VMEM((32, 576, 256), BF),
            pltpu.VMEM((16, 512, 128), BF),
            pltpu.VMEM((32, 576), F32),
            pltpu.VMEM((16, 16, 512), F32),
            pltpu.VMEM((2, 2, 16, 1024), BF),
            pltpu.VMEM((2, 512, 896), BF),
            pltpu.VMEM((2, 576, 896), BF),
            pltpu.VMEM((2, 576, 896), BF),
            pltpu.VMEM((2, 576, 896), BF),
            pltpu.VMEM((8, 2, 2, 16, 1024), BF),
            pltpu.VMEM((2, 16, 16, 1024), BF),
            plane, plane, plane, plane,
            pltpu.VMEM((2, 2, 8, 128), F32),
            pltpu.VMEM((2, 8, 8, 128), F32),
            pltpu.VMEM((2, 128, 128), F32),
            pltpu.VMEM((2, 2, 8, 32, 1152), F32),
            pltpu.VMEM((2, 2, 32, 1152), BF),
            pltpu.VMEM((2, 2, 4, 2, 32, 1152), BF),
            pltpu.VMEM((2, 8, 2, 16, 1152), BF),
            plane, plane,
            dma((GROUPS,)), dma,
            dma((4,)), dma((4,)), dma((4,)),
            dma((2, 2, 4, 2)), dma((2, 2, 4, 2)),
            dma((2, 16)), dma((2, 16)),
            dma((2, 16)), dma((2, 16)),
            dma((2, 16)), dma((2, 16)),
            dma((2, 8)), dma((2, 8)),
            dma((2, 2, 4, 2)), dma((2, 2, 4, 2)),
            dma((2, 2, 4, 2)), dma((2, 2, 4, 2)),
            dma((2, 16)), dma((2, 16)),
        ],
        compiler_params=pltpu.CompilerParams(
            collective_id=0, has_side_effects=True, vmem_limit_bytes=56 * 2**20
        ),
        name="layer",
    )(lengths, q_full, fresh, cache, value_up, out_proj, residual, gain, gate, up, down)


def body(
    queries,
    latent_cache,
    fresh_latent_entry,
    lengths,
    key_up_matrix,
    value_up_matrix,
    out_proj,
    residual,
    norm_gain,
    gate_weight,
    up_weight,
    down_weight,
):
    query_heads = queries.reshape(32, 16, 192)
    q_latent = jnp.einsum(
        "rhk,hkl->rhl", query_heads[:, :, :128], key_up_matrix, preferred_element_type=F32
    ).astype(BF)
    q_full = jnp.concatenate([q_latent, query_heads[:, :, 128:]], axis=2)
    return layer(
        lengths,
        q_full,
        fresh_latent_entry,
        latent_cache.transpose(0, 2, 1),
        value_up_matrix,
        out_proj,
        residual,
        norm_gain.reshape(1, -1),
        gate_weight.T,
        up_weight.T,
        down_weight,
    )


def solution(mesh):
    return jax.shard_map(
        body,
        mesh=mesh,
        in_specs=(
            P("dp", "tp"),
            P("dp", None, None),
            P("dp", None),
            P("dp"),
            P("tp", None, None),
            P("tp", None, None),
            P("dp", "tp"),
            P("dp", "tp"),
            P("tp"),
            P("tp", "dp"),
            P("tp", "dp"),
            P("dp", "tp"),
        ),
        out_specs=P("dp", "tp"),
        check_vma=False,
    )
```

```python
import jax
import jax.numpy as jnp
from jax import lax
from jax.experimental import pallas as pl
from jax.experimental.pallas import tpu as pltpu
from jax.sharding import PartitionSpec as P

MESH = pl.DeviceIdType.MESH
BF = jnp.bfloat16
F32 = jnp.float32
D = 7168
EPS = 1e-06
GROUP = 8
GROUPS = 4
SCALE = 1.0 / 192**0.5


def layer_kernel(
    lengths, q_full, fresh, cache, value_up, out_proj, residual, gain, gate, up, down,
    out,
    keys, vup, fresh_f, lat, attn, wo, wg, wu, wd, zbuf, ain, proj, rs1, sg, xn, st, stin, rcol, own, p4, z6, hid, dnb, rs2,
    c_s, v_s, w_l, w_s, w_r, z_s, z_r, a_s, a_r, p_s, p_r, g_s, g_r, t_s, t_r, z6_s, z6_r, h_s, h_r, d_s, d_r,
):
    dp = lax.axis_index("dp")
    k = lax.axis_index("tp")
    c = dp % 2
    p = dp // 2

    def chip(q):
        return (2 * q + c, k)

    def level(delta):
        return (dp, (k + 8 + delta) % 8)

    partner = (2 * p + 1 - c, k)
    dirs = (1, -1)
    leaving = []

    def remote(src, dst, ssem, rsem, dev):
        return pltpu.make_async_remote_copy(
            src_ref=src, dst_ref=dst, send_sem=ssem, recv_sem=rsem, device_id=dev, device_id_type=MESH
        )

    def send(src, dst, ssem, rsem, dev):
        remote(src, dst, ssem, rsem, dev).start()
        leaving.append((src, ssem))

    def arrived(ref, sem):
        pltpu.make_async_copy(ref, ref, sem).wait()

    barrier = pltpu.get_barrier_semaphore()
    pl.semaphore_signal(barrier, inc=1, device_id=partner, device_id_type=MESH)

    def greet_plane(d, _):
        pl.semaphore_signal(barrier, inc=1, device_id=chip((p + d) % 16), device_id_type=MESH)
        return 0

    lax.fori_loop(1, 16, greet_plane, 0)

    def greet_level(d, _):
        pl.semaphore_signal(barrier, inc=1, device_id=level(d), device_id_type=MESH)
        return 0

    lax.fori_loop(1, 8, greet_level, 0)

    for g in range(GROUPS):
        rows = pl.ds(g * GROUP, GROUP)
        pltpu.make_async_copy(cache.at[rows], keys.at[rows], c_s.at[g]).start()
        if g == 1:
            pltpu.make_async_copy(value_up, vup, v_s).start()
    pairs = ((out_proj, wo.at[c]), (gate, wg.at[c]), (up, wu.at[c]), (down, wd.at[c]))
    theirs = (wo.at[1 - c], wg.at[1 - c], wu.at[1 - c], wd.at[1 - c])
    for n, (src, dst) in enumerate(pairs):
        pltpu.make_async_copy(src, dst, w_l.at[n]).start()
    fresh_f[...] = fresh[...].astype(F32)

    def weight(n):
        pltpu.make_async_copy(pairs[n][0], pairs[n][1], w_l.at[n]).wait()
        arrived(theirs[n], w_r.at[n])

    slot = lax.broadcasted_iota(jnp.int32, (16, 256), 1)

    def attend(g):
        arrived(keys.at[pl.ds(g * GROUP, GROUP)], c_s.at[g])
        scores, new_score, used = [], [], []
        for i in range(GROUP):
            r = g * GROUP + i
            q = q_full[r]
            entry = fresh_f[pl.ds(r, 1), :]
            scores.append(jnp.dot(q, keys[r], preferred_element_type=F32) * SCALE)
            new_score.append(jnp.sum(q.astype(F32) * entry, axis=1, keepdims=True) * SCALE)
            used.append(slot < lengths[r])
        masked = jnp.concatenate([jnp.where(u, v, -1e30) for u, v in zip(used, scores)], axis=0)
        new_score = jnp.concatenate(new_score, axis=0)
        top = jnp.maximum(jnp.max(masked, axis=1, keepdims=True), new_score)
        powers = jnp.exp(masked - top)
        weights = jnp.concatenate(
            [jnp.where(u, powers[16 * i : 16 * i + 16], 0.0) for i, u in enumerate(used)], axis=0
        )
        new_weight = jnp.exp(new_score - top)
        denom = jnp.sum(weights, axis=1, keepdims=True) + new_weight
        probs = (weights / denom).astype(BF)
        new_prob = (new_weight / denom).astype(BF).astype(F32)
        for i in range(GROUP):
            r = g * GROUP + i
            own_rows = slice(16 * i, 16 * i + 16)
            res = lax.dot_general(
                probs[own_rows], keys[r, 0:512, :], (((1,), (1,)), ((), ())), preferred_element_type=F32
            )
            lat[:, r % 16, :] = res + new_prob[own_rows] * fresh_f[pl.ds(r, 1), 0:512]

    def attend_groups(first, last):
        lax.fori_loop(first, last, lambda g, _: (attend(g), 0)[1], 0)

    def heads_out(ch):
        def head(h, _):
            res = jnp.dot(lat[h].astype(BF), vup[h], preferred_element_type=F32)
            attn[h // 8, ch, :, pl.ds(pl.multiple_of((h % 8) * 128, 128), 128)] = res.astype(BF)
            return 0

        lax.fori_loop(0, 16, head, 0, unroll=4)

    def to_rows(blk, b, ch, ref):
        q = 2 * blk + b

        @pl.when(q != p)
        def _():
            remote(ref, ain.at[ch, p], a_s.at[ch, q], a_r.at[ch, p], chip(q)).start()

        @pl.when(q == p)
        def _():
            pltpu.make_async_copy(ref, ain.at[ch, p], a_r.at[ch, p]).start()

    def heads_start(ch):
        for hop in (2, 1):
            for b in range(2):
                for di, d in enumerate(dirs):
                    send(
                        attn.at[b, ch], zbuf.at[k, b, ch],
                        z_s.at[ch, di, hop - 1, b], z_r.at[ch, di, hop - 1, b], level(hop * d),
                    )
        for b in range(2):
            to_rows(k, b, ch, attn.at[b, ch])

    def heads_mid(ch):
        for b in range(2):
            for di, d in enumerate(dirs):
                blk = (k + 8 - 2 * d) % 8
                ref = zbuf.at[blk, b, ch]
                arrived(ref, z_r.at[ch, di, 1, b])
                send(ref, ref, z_s.at[ch, di, 2, b], z_r.at[ch, di, 2, b], level(d))
                if b == di:
                    send(ref, ref, z_s.at[ch, di, 3, b], z_r.at[ch, di, 3, b], level(2 * d))
        for hop in (2, 1):
            for b in range(2):
                for di, d in enumerate(dirs):
                    blk = (k + 8 - hop * d) % 8
                    ref = zbuf.at[blk, b, ch]
                    if hop == 1:
                        arrived(ref, z_r.at[ch, di, 0, b])
                    to_rows(blk, b, ch, ref)

    def heads_end(ch):
        for hop in (3, 4):
            for b in range(2):
                for di, d in enumerate(dirs):
                    if hop == 4 and b != di:
                        continue
                    blk = (k + 8 - hop * d) % 8
                    ref = zbuf.at[blk, b, ch]
                    arrived(ref, z_r.at[ch, di, hop - 1, b])
                    to_rows(blk, b, ch, ref)

    def swap():
        pl.semaphore_wait(barrier, 23)
        for n, (src, dst) in enumerate(pairs):
            send(src, dst, w_s.at[n], w_r.at[n], partner)

    def project(ch, send_now):
        def group(g, _):
            first = (((p // 8) + 1 + g) % 2) * 8

            def wait_rows(j, _):
                arrived(ain.at[ch, first + j], a_r.at[ch, first + j])
                return 0

            lax.fori_loop(0, 8, wait_rows, 0)
            rows = ain[ch, pl.ds(first, 8)].reshape(128, 1024)
            part = jnp.dot(rows, wo[...].reshape(1024, 896), preferred_element_type=F32)
            proj[ch, pl.ds(first, 8)] = part.astype(BF).reshape(8, 16, 896)
            if send_now:
                for j in range(8):

                    @pl.when(first + j != p)
                    def _():
                        q = first + j
                        remote(proj.at[ch, q], rs1.at[ch, p], p_s.at[ch, q], p_r.at[ch, p], chip(q)).start()

            return 0

        lax.fori_loop(0, 2, group, 0)

    def send_proj(ch):
        def one(d, _):
            q = (p + d) % 16
            remote(proj.at[ch, q], rs1.at[ch, p], p_s.at[ch, q], p_r.at[ch, p], chip(q)).start()
            return 0

        lax.fori_loop(1, 16, one, 0)

    def join(ch):
        def add(d, acc):
            q = (p + d) % 16
            arrived(rs1.at[ch, q], p_r.at[ch, q])
            return acc + rs1[ch, q].astype(F32)

        total = residual[16 * ch : 16 * ch + 16].astype(F32) + proj[ch, p].astype(F32)
        sg[ch, p] = lax.fori_loop(1, 16, add, total).astype(BF)

        def spread(d, _):
            q = (p + d) % 16
            remote(sg.at[ch, p], sg.at[ch, p], g_s.at[ch, q], g_r.at[ch, p], chip(q)).start()
            return 0

        lax.fori_loop(1, 16, spread, 0)

    f = p // 2
    kk = (k + f) % 8

    def lab(delta):
        return (kk + 8 + delta) % 8

    def expand(ch):
        def gathered(d, _):
            q = (p + d) % 16
            arrived(sg.at[ch, q], g_r.at[ch, q])
            return 0

        lax.fori_loop(1, 16, gathered, 0)
        gain_f = gain[...].astype(F32).reshape(1, 896)

        def scale(g, _):
            s = sg[ch, pl.ds(8 * g, 8)].reshape(128, 896).astype(F32)
            xn[ch, pl.ds(8 * g, 8)] = (s * gain_f).astype(BF).reshape(8, 16, 896)
            sq = s * s
            lanes = sq[:, 0:128]
            for i in range(1, 7):
                lanes = lanes + sq[:, 128 * i : 128 * i + 128]
            st[ch, g] = jnp.broadcast_to(jnp.sum(jnp.transpose(lanes), axis=0, keepdims=True), (8, 128))
            return 0

        lax.fori_loop(0, 2, scale, 0)
        rows = xn[ch].reshape(256, 896)
        for h, w in enumerate((wg, wu)):
            res = lax.dot_general(
                rows, w[...].reshape(1152, 896), (((1,), (1,)), ((), ())), preferred_element_type=F32
            )
            own[ch, h] = res.reshape(8, 32, 1152)
            p4[ch, h] = own[ch, h, lab(4)].astype(BF)
            send(
                p4.at[ch, h], z6.at[ch, h, 0, h], z6_s.at[ch, h, 0, h], z6_r.at[ch, h, 0, h], level(dirs[h])
            )

        def send_stat(d, _):
            remote(
                st.at[ch, lab(d) // 4], stin.at[ch, d], t_s.at[ch, d], t_r.at[ch, d], level(d)
            ).start()
            return 0

        lax.fori_loop(1, 8, send_stat, 0)

    def chain(ch, t):
        for h in range(2):
            for di, d in enumerate(dirs):
                ref = z6.at[ch, di, t - 1, h]
                mine = own[ch, h, lab(d * (4 - t))]
                if h == di or t > 1:
                    arrived(ref, z6_r.at[ch, di, t - 1, h])
                    mine = mine + z6[ch, di, t - 1, h].astype(F32)
                z6[ch, di, t - 1, h] = mine.astype(BF)
                send(ref, z6.at[ch, di, t, h], z6_s.at[ch, di, t, h], z6_r.at[ch, di, t, h], level(d))

    def lower(ch, labs):
        n = 32 * len(labs)
        rows = [hid[ch, l].reshape(32, 1152) for l in labs]
        rows = rows[0] if len(labs) == 1 else jnp.concatenate(rows, axis=0)
        part = jnp.dot(rows, wd[...].reshape(1152, 896), preferred_element_type=F32).astype(BF)
        for i, l in enumerate(labs):
            dnb[ch, pl.ds(2 * l, 2)] = part[32 * i : 32 * i + 32].reshape(2, 16, 896)
            for b in range(2):
                q = 2 * l + b

                @pl.when(q != p)
                def _():
                    remote(dnb.at[ch, q], rs2.at[ch, p], d_s.at[ch, q], d_r.at[ch, p], chip(q)).start()

    def activate(ch):
        def add_stat(d, acc):
            arrived(stin.at[ch, d], t_r.at[ch, d])
            return acc + stin[ch, d]

        square = lax.fori_loop(1, 8, add_stat, st[ch, kk // 4])

        def sent_stat(d, _):
            pltpu.make_async_copy(stin.at[ch, d], stin.at[ch, d], t_s.at[ch, d]).wait()
            return 0

        lax.fori_loop(1, 8, sent_stat, 0)
        inv = lax.rsqrt(square / D + EPS)
        rcol[ch] = jnp.transpose(jnp.broadcast_to(inv[0:1, :], (128, 128)))
        r = rcol[ch, pl.ds(pl.multiple_of((kk % 4) * 32, 32), 32), :][:, 0:1]
        sums = []
        for h in range(2):
            for di in range(2):
                arrived(z6.at[ch, di, 3, h], z6_r.at[ch, di, 3, h])
            total = own[ch, h, kk] + z6[ch, 0, 3, h].astype(F32) + z6[ch, 1, 3, h].astype(F32)
            sums.append(total * r)
        units = sums[0] / (1.0 + jnp.exp(-sums[0])) * sums[1]
        hid[ch, kk] = units.astype(BF).reshape(2, 16, 1152)
        for hop in (2, 1):
            for di, d in enumerate(dirs):
                for b in range(2):
                    ref = hid.at[ch, kk, b]
                    send(ref, ref, h_s.at[ch, di, hop - 1, b], h_r.at[ch, di, hop - 1, b], level(hop * d))

    def collect_mid(ch):
        for b in range(2):
            for di, d in enumerate(dirs):
                ref = hid.at[ch, lab(-2 * d), b]
                arrived(ref, h_r.at[ch, di, 1, b])
                send(ref, ref, h_s.at[ch, di, 2, b], h_r.at[ch, di, 2, b], level(d))
                if b == di:
                    send(ref, ref, h_s.at[ch, di, 3, b], h_r.at[ch, di, 3, b], level(2 * d))
        for b in range(2):
            for di, d in enumerate(dirs):
                arrived(hid.at[ch, lab(-d), b], h_r.at[ch, di, 0, b])

    def collect_end(ch):
        for hop in (3, 4):
            for b in range(2):
                for di, d in enumerate(dirs):
                    if hop == 3 or b == di:
                        arrived(hid.at[ch, lab(-hop * d), b], h_r.at[ch, di, hop - 1, b])

    def settle(kinds, chunks):
        def one(d, _):
            q = (p + d) % 16
            for ch in chunks:
                for ref, sem in kinds:
                    pltpu.make_async_copy(ref.at[ch, q], ref.at[ch, q], sem.at[ch, q]).wait()
            return 0

        lax.fori_loop(1, 16, one, 0)

    def settle_all():
        for ref, sem in leaving:
            pltpu.make_async_copy(ref, ref, sem).wait()
        leaving.clear()

    def finish(ch):
        def add(d, acc):
            q = (p + d) % 16
            arrived(rs2.at[ch, q], d_r.at[ch, q])
            return acc + rs2[ch, q].astype(F32)

        total = sg[ch, p].astype(F32) + dnb[ch, p].astype(F32)
        out[16 * ch : 16 * ch + 16] = lax.fori_loop(1, 16, add, total).astype(BF)

    attend_groups(0, 1)
    swap()
    attend_groups(1, 2)
    pltpu.make_async_copy(value_up, vup, v_s).wait()
    heads_out(0)
    heads_start(0)
    attend_groups(2, 4)
    heads_mid(0)
    heads_out(1)
    heads_start(1)
    weight(0)
    heads_end(0)
    heads_mid(1)
    project(0, True)
    heads_end(1)
    project(1, False)
    join(0)
    send_proj(1)
    weight(1)
    weight(2)
    expand(0)
    join(1)
    chain(0, 1)
    chain(0, 2)
    expand(1)
    chain(0, 3)
    chain(1, 1)
    activate(0)
    chain(1, 2)
    weight(3)
    lower(0, [kk])
    settle(((ain, a_s), (proj, p_s), (sg, g_s)), (0, 1))
    collect_mid(0)
    chain(1, 3)
    lower(0, [lab(1), lab(-1), lab(2), lab(-2)])
    collect_end(0)
    activate(1)
    lower(0, [lab(3), lab(-3), lab(4)])
    lower(1, [kk])
    settle_all()
    collect_mid(1)
    lower(1, [lab(1), lab(-1), lab(2), lab(-2)])
    settle(((dnb, d_s),), (0,))
    finish(0)
    collect_end(1)
    lower(1, [lab(3), lab(-3), lab(4)])
    settle_all()
    finish(1)
    settle(((dnb, d_s),), (1,))


def layer(lengths, q_full, fresh, cache, value_up, out_proj, residual, gain, gate, up, down):
    vm = pl.BlockSpec(memory_space=pltpu.VMEM)
    hbm = pl.BlockSpec(memory_space=pl.ANY)
    dma = pltpu.SemaphoreType.DMA
    plane = pltpu.VMEM((2, 16, 16, 896), BF)
    return pl.pallas_call(
        layer_kernel,
        out_shape=jax.ShapeDtypeStruct((32, 896), BF),
        in_specs=[pl.BlockSpec(memory_space=pltpu.SMEM), vm, vm, hbm, hbm, hbm, vm, vm, hbm, hbm, hbm],
        out_specs=vm,
        scratch_shapes=[
            pltpu.VMEM((32, 576, 256), BF),
            pltpu.VMEM((16, 512, 128), BF),
            pltpu.VMEM((32, 576), F32),
            pltpu.VMEM((16, 16, 512), F32),
            pltpu.VMEM((2, 2, 16, 1024), BF),
            pltpu.VMEM((2, 512, 896), BF),
            pltpu.VMEM((2, 576, 896), BF),
            pltpu.VMEM((2, 576, 896), BF),
            pltpu.VMEM((2, 576, 896), BF),
            pltpu.VMEM((8, 2, 2, 16, 1024), BF),
            pltpu.VMEM((2, 16, 16, 1024), BF),
            plane, plane, plane, plane,
            pltpu.VMEM((2, 2, 8, 128), F32),
            pltpu.VMEM((2, 8, 8, 128), F32),
            pltpu.VMEM((2, 128, 128), F32),
            pltpu.VMEM((2, 2, 8, 32, 1152), F32),
            pltpu.VMEM((2, 2, 32, 1152), BF),
            pltpu.VMEM((2, 2, 4, 2, 32, 1152), BF),
            pltpu.VMEM((2, 8, 2, 16, 1152), BF),
            plane, plane,
            dma((GROUPS,)), dma,
            dma((4,)), dma((4,)), dma((4,)),
            dma((2, 2, 4, 2)), dma((2, 2, 4, 2)),
            dma((2, 16)), dma((2, 16)),
            dma((2, 16)), dma((2, 16)),
            dma((2, 16)), dma((2, 16)),
            dma((2, 8)), dma((2, 8)),
            dma((2, 2, 4, 2)), dma((2, 2, 4, 2)),
            dma((2, 2, 4, 2)), dma((2, 2, 4, 2)),
            dma((2, 16)), dma((2, 16)),
        ],
        compiler_params=pltpu.CompilerParams(
            collective_id=0, has_side_effects=True, vmem_limit_bytes=53 * 2**20
        ),
        name="layer",
    )(lengths, q_full, fresh, cache, value_up, out_proj, residual, gain, gate, up, down)


def body(
    queries,
    latent_cache,
    fresh_latent_entry,
    lengths,
    key_up_matrix,
    value_up_matrix,
    out_proj,
    residual,
    norm_gain,
    gate_weight,
    up_weight,
    down_weight,
):
    query_heads = queries.reshape(32, 16, 192)
    q_latent = jnp.einsum(
        "rhk,hkl->rhl", query_heads[:, :, :128], key_up_matrix, preferred_element_type=F32
    ).astype(BF)
    q_full = jnp.concatenate([q_latent, query_heads[:, :, 128:]], axis=2)
    return layer(
        lengths,
        q_full,
        fresh_latent_entry,
        latent_cache.transpose(0, 2, 1),
        value_up_matrix,
        out_proj,
        residual,
        norm_gain,
        gate_weight.T,
        up_weight.T,
        down_weight,
    )


def solution(mesh):
    return jax.shard_map(
        body,
        mesh=mesh,
        in_specs=(
            P("dp", "tp"),
            P("dp", None, None),
            P("dp", None),
            P("dp"),
            P("tp", None, None),
            P("tp", None, None),
            P("dp", "tp"),
            P("dp", "tp"),
            P("tp"),
            P("tp", "dp"),
            P("tp", "dp"),
            P("dp", "tp"),
        ),
        out_specs=P("dp", "tp"),
        check_vma=False,
    )
```

```python
import jax
import jax.numpy as jnp
from jax import lax
from jax.experimental import pallas as pl
from jax.experimental.pallas import tpu as pltpu
from jax.sharding import PartitionSpec as P

MESH = pl.DeviceIdType.MESH
BF = jnp.bfloat16
F32 = jnp.float32
D = 7168
EPS = 1e-06
GROUP = 8
GROUPS = 4
SCALE = 1.0 / 192**0.5


def layer_kernel(
    lengths, q_latent, q_heads, fresh, cache, value_up, out_proj, residual, gain, gate, up, down,
    out,
    keys, vup, fresh_f, lat, attn, wo, wg, wu, wd, zbuf, ain, proj, rs1, sg, xn, st, stin, rcol, own, p4, z6, hid, dnb, rs2,
    c_s, v_s, w_l, w_s, w_r, z_s, z_r, a_s, a_r, p_s, p_r, g_s, g_r, t_s, t_r, z6_s, z6_r, h_s, h_r, d_s, d_r,
):
    dp = lax.axis_index("dp")
    k = lax.axis_index("tp")
    c = dp % 2
    p = dp // 2

    def chip(q):
        return (2 * q + c, k)

    def level(delta):
        return (dp, (k + 8 + delta) % 8)

    partner = (2 * p + 1 - c, k)
    dirs = (1, -1)
    leaving = []

    def remote(src, dst, ssem, rsem, dev):
        return pltpu.make_async_remote_copy(
            src_ref=src, dst_ref=dst, send_sem=ssem, recv_sem=rsem, device_id=dev, device_id_type=MESH
        )

    def send(src, dst, ssem, rsem, dev):
        remote(src, dst, ssem, rsem, dev).start()
        leaving.append((src, ssem))

    def arrived(ref, sem):
        pltpu.make_async_copy(ref, ref, sem).wait()

    for g in range(GROUPS):
        rows = pl.ds(g * GROUP, GROUP)
        pltpu.make_async_copy(cache.at[rows], keys.at[rows], c_s.at[g]).start()
        if g == 1:
            pltpu.make_async_copy(value_up, vup, v_s).start()
    pairs = ((out_proj, wo.at[c]), (gate, wg.at[c]), (up, wu.at[c]), (down, wd.at[c]))
    theirs = (wo.at[1 - c], wg.at[1 - c], wu.at[1 - c], wd.at[1 - c])
    for n, (src, dst) in enumerate(pairs):
        pltpu.make_async_copy(src, dst, w_l.at[n]).start()

    barrier = pltpu.get_barrier_semaphore()
    pl.semaphore_signal(barrier, inc=1, device_id=partner, device_id_type=MESH)

    def greet_plane(d, _):
        pl.semaphore_signal(barrier, inc=1, device_id=chip((p + d) % 16), device_id_type=MESH)
        return 0

    lax.fori_loop(1, 16, greet_plane, 0)

    def greet_level(d, _):
        pl.semaphore_signal(barrier, inc=1, device_id=level(d), device_id_type=MESH)
        return 0

    lax.fori_loop(1, 8, greet_level, 0)

    fresh_f[...] = fresh[...].astype(F32)

    def weight(n):
        pltpu.make_async_copy(pairs[n][0], pairs[n][1], w_l.at[n]).wait()
        arrived(theirs[n], w_r.at[n])

    slot = lax.broadcasted_iota(jnp.int32, (16, 256), 1)

    def attend(g):
        arrived(keys.at[pl.ds(g * GROUP, GROUP)], c_s.at[g])
        scores, new_score, used = [], [], []
        for i in range(GROUP):
            r = g * GROUP + i
            q = q_latent[r]
            turned = q_heads[r, :, 128:192]
            entry = fresh_f[pl.ds(r, 1), :]
            score = jnp.dot(q, keys[r, 0:512, :], preferred_element_type=F32) + jnp.dot(
                turned, keys[r, 512:576, :], preferred_element_type=F32
            )
            scores.append(score * SCALE)
            fresh_score = jnp.sum(q.astype(F32) * entry[:, 0:512], axis=1, keepdims=True) + jnp.sum(
                turned.astype(F32) * entry[:, 512:576], axis=1, keepdims=True
            )
            new_score.append(fresh_score * SCALE)
            used.append(slot < lengths[r])
        masked = jnp.concatenate([jnp.where(u, v, -1e30) for u, v in zip(used, scores)], axis=0)
        new_score = jnp.concatenate(new_score, axis=0)
        top = jnp.maximum(jnp.max(masked, axis=1, keepdims=True), new_score)
        powers = jnp.exp(masked - top)
        weights = jnp.concatenate(
            [jnp.where(u, powers[16 * i : 16 * i + 16], 0.0) for i, u in enumerate(used)], axis=0
        )
        new_weight = jnp.exp(new_score - top)
        denom = jnp.sum(weights, axis=1, keepdims=True) + new_weight
        probs = (weights / denom).astype(BF)
        new_prob = (new_weight / denom).astype(BF).astype(F32)
        for i in range(GROUP):
            r = g * GROUP + i
            own_rows = slice(16 * i, 16 * i + 16)
            res = lax.dot_general(
                probs[own_rows], keys[r, 0:512, :], (((1,), (1,)), ((), ())), preferred_element_type=F32
            )
            lat[:, r % 16, :] = res + new_prob[own_rows] * fresh_f[pl.ds(r, 1), 0:512]

    def attend_groups(first, last):
        lax.fori_loop(first, last, lambda g, _: (attend(g), 0)[1], 0)

    def heads_out(ch):
        def head(h, _):
            res = jnp.dot(lat[h].astype(BF), vup[h], preferred_element_type=F32)
            attn[h // 8, ch, :, pl.ds(pl.multiple_of((h % 8) * 128, 128), 128)] = res.astype(BF)
            return 0

        lax.fori_loop(0, 16, head, 0, unroll=4)

    def to_rows(blk, b, ch, ref):
        q = 2 * blk + b

        @pl.when(q != p)
        def _():
            remote(ref, ain.at[ch, p], a_s.at[ch, q], a_r.at[ch, p], chip(q)).start()

        @pl.when(q == p)
        def _():
            pltpu.make_async_copy(ref, ain.at[ch, p], a_r.at[ch, p]).start()

    def heads_start(ch):
        for hop in (2, 1):
            for b in range(2):
                for di, d in enumerate(dirs):
                    send(
                        attn.at[b, ch], zbuf.at[k, b, ch],
                        z_s.at[ch, di, hop - 1, b], z_r.at[ch, di, hop - 1, b], level(hop * d),
                    )
        for b in range(2):
            to_rows(k, b, ch, attn.at[b, ch])

    def heads_mid(ch):
        for b in range(2):
            for di, d in enumerate(dirs):
                blk = (k + 8 - 2 * d) % 8
                ref = zbuf.at[blk, b, ch]
                arrived(ref, z_r.at[ch, di, 1, b])
                send(ref, ref, z_s.at[ch, di, 2, b], z_r.at[ch, di, 2, b], level(d))
                if b == di:
                    send(ref, ref, z_s.at[ch, di, 3, b], z_r.at[ch, di, 3, b], level(2 * d))
        for hop in (2, 1):
            for b in range(2):
                for di, d in enumerate(dirs):
                    blk = (k + 8 - hop * d) % 8
                    ref = zbuf.at[blk, b, ch]
                    if hop == 1:
                        arrived(ref, z_r.at[ch, di, 0, b])
                    to_rows(blk, b, ch, ref)

    def heads_end(ch):
        for hop in (3, 4):
            for b in range(2):
                for di, d in enumerate(dirs):
                    if hop == 4 and b != di:
                        continue
                    blk = (k + 8 - hop * d) % 8
                    ref = zbuf.at[blk, b, ch]
                    arrived(ref, z_r.at[ch, di, hop - 1, b])
                    to_rows(blk, b, ch, ref)

    def swap():
        pl.semaphore_wait(barrier, 23)
        for n, (src, dst) in enumerate(pairs):
            send(src, dst, w_s.at[n], w_r.at[n], partner)

    def project(ch, send_now):
        def group(g, _):
            first = (((p // 8) + 1 + g) % 2) * 8

            def wait_rows(j, _):
                arrived(ain.at[ch, first + j], a_r.at[ch, first + j])
                return 0

            lax.fori_loop(0, 8, wait_rows, 0)
            rows = ain[ch, pl.ds(first, 8)].reshape(128, 1024)
            part = jnp.dot(rows, wo[...].reshape(1024, 896), preferred_element_type=F32)
            proj[ch, pl.ds(first, 8)] = part.astype(BF).reshape(8, 16, 896)
            if send_now:
                for j in range(8):

                    @pl.when(first + j != p)
                    def _():
                        q = first + j
                        remote(proj.at[ch, q], rs1.at[ch, p], p_s.at[ch, q], p_r.at[ch, p], chip(q)).start()

            return 0

        lax.fori_loop(0, 2, group, 0)

    def send_proj(ch):
        def one(d, _):
            q = (p + d) % 16
            remote(proj.at[ch, q], rs1.at[ch, p], p_s.at[ch, q], p_r.at[ch, p], chip(q)).start()
            return 0

        lax.fori_loop(1, 16, one, 0)

    def join(ch):
        def add(d, acc):
            q = (p + d) % 16
            arrived(rs1.at[ch, q], p_r.at[ch, q])
            return acc + rs1[ch, q].astype(F32)

        total = residual[16 * ch : 16 * ch + 16].astype(F32) + proj[ch, p].astype(F32)
        sg[ch, p] = lax.fori_loop(1, 16, add, total).astype(BF)

        def spread(d, _):
            q = (p + d) % 16
            remote(sg.at[ch, p], sg.at[ch, p], g_s.at[ch, q], g_r.at[ch, p], chip(q)).start()
            return 0

        lax.fori_loop(1, 16, spread, 0)

    f = p // 2
    kk = (k + f) % 8

    def lab(delta):
        return (kk + 8 + delta) % 8

    def expand(ch):
        def gathered(d, _):
            q = (p + d) % 16
            arrived(sg.at[ch, q], g_r.at[ch, q])
            return 0

        lax.fori_loop(1, 16, gathered, 0)
        gain_f = gain[...].astype(F32).reshape(1, 896)

        def scale(g, _):
            s = sg[ch, pl.ds(8 * g, 8)].reshape(128, 896).astype(F32)
            xn[ch, pl.ds(8 * g, 8)] = (s * gain_f).astype(BF).reshape(8, 16, 896)
            sq = s * s
            lanes = sq[:, 0:128]
            for i in range(1, 7):
                lanes = lanes + sq[:, 128 * i : 128 * i + 128]
            st[ch, g] = jnp.broadcast_to(jnp.sum(jnp.transpose(lanes), axis=0, keepdims=True), (8, 128))
            return 0

        lax.fori_loop(0, 2, scale, 0)
        rows = xn[ch].reshape(256, 896)
        for h, w in enumerate((wg, wu)):
            res = lax.dot_general(
                rows, w[...].reshape(1152, 896), (((1,), (1,)), ((), ())), preferred_element_type=F32
            )
            own[ch, h] = res.reshape(8, 32, 1152)
            p4[ch, h] = own[ch, h, lab(4)].astype(BF)
            send(
                p4.at[ch, h], z6.at[ch, h, 0, h], z6_s.at[ch, h, 0, h], z6_r.at[ch, h, 0, h], level(dirs[h])
            )

        def send_stat(d, _):
            remote(
                st.at[ch, lab(d) // 4], stin.at[ch, d], t_s.at[ch, d], t_r.at[ch, d], level(d)
            ).start()
            return 0

        lax.fori_loop(1, 8, send_stat, 0)

    def chain(ch, t):
        for h in range(2):
            for di, d in enumerate(dirs):
                ref = z6.at[ch, di, t - 1, h]
                mine = own[ch, h, lab(d * (4 - t))]
                if h == di or t > 1:
                    arrived(ref, z6_r.at[ch, di, t - 1, h])
                    mine = mine + z6[ch, di, t - 1, h].astype(F32)
                z6[ch, di, t - 1, h] = mine.astype(BF)
                send(ref, z6.at[ch, di, t, h], z6_s.at[ch, di, t, h], z6_r.at[ch, di, t, h], level(d))

    def lower(ch, labs):
        n = 32 * len(labs)
        rows = [hid[ch, l].reshape(32, 1152) for l in labs]
        rows = rows[0] if len(labs) == 1 else jnp.concatenate(rows, axis=0)
        part = jnp.dot(rows, wd[...].reshape(1152, 896), preferred_element_type=F32).astype(BF)
        for i, l in enumerate(labs):
            dnb[ch, pl.ds(2 * l, 2)] = part[32 * i : 32 * i + 32].reshape(2, 16, 896)
            for b in range(2):
                q = 2 * l + b

                @pl.when(q != p)
                def _():
                    remote(dnb.at[ch, q], rs2.at[ch, p], d_s.at[ch, q], d_r.at[ch, p], chip(q)).start()

    def activate(ch):
        def add_stat(d, acc):
            arrived(stin.at[ch, d], t_r.at[ch, d])
            return acc + stin[ch, d]

        square = lax.fori_loop(1, 8, add_stat, st[ch, kk // 4])

        def sent_stat(d, _):
            pltpu.make_async_copy(stin.at[ch, d], stin.at[ch, d], t_s.at[ch, d]).wait()
            return 0

        lax.fori_loop(1, 8, sent_stat, 0)
        inv = lax.rsqrt(square / D + EPS)
        rcol[ch] = jnp.transpose(jnp.broadcast_to(inv[0:1, :], (128, 128)))
        r = rcol[ch, pl.ds(pl.multiple_of((kk % 4) * 32, 32), 32), :][:, 0:1]
        sums = []
        for h in range(2):
            for di in range(2):
                arrived(z6.at[ch, di, 3, h], z6_r.at[ch, di, 3, h])
            total = own[ch, h, kk] + z6[ch, 0, 3, h].astype(F32) + z6[ch, 1, 3, h].astype(F32)
            sums.append(total * r)
        units = sums[0] / (1.0 + jnp.exp(-sums[0])) * sums[1]
        hid[ch, kk] = units.astype(BF).reshape(2, 16, 1152)
        for hop in (2, 1):
            for di, d in enumerate(dirs):
                for b in range(2):
                    ref = hid.at[ch, kk, b]
                    send(ref, ref, h_s.at[ch, di, hop - 1, b], h_r.at[ch, di, hop - 1, b], level(hop * d))

    def collect_mid(ch):
        for b in range(2):
            for di, d in enumerate(dirs):
                ref = hid.at[ch, lab(-2 * d), b]
                arrived(ref, h_r.at[ch, di, 1, b])
                send(ref, ref, h_s.at[ch, di, 2, b], h_r.at[ch, di, 2, b], level(d))
                if b == di:
                    send(ref, ref, h_s.at[ch, di, 3, b], h_r.at[ch, di, 3, b], level(2 * d))
        for b in range(2):
            for di, d in enumerate(dirs):
                arrived(hid.at[ch, lab(-d), b], h_r.at[ch, di, 0, b])

    def collect_end(ch):
        for hop in (3, 4):
            for b in range(2):
                for di, d in enumerate(dirs):
                    if hop == 3 or b == di:
                        arrived(hid.at[ch, lab(-hop * d), b], h_r.at[ch, di, hop - 1, b])

    def settle(kinds, chunks):
        def one(d, _):
            q = (p + d) % 16
            for ch in chunks:
                for ref, sem in kinds:
                    pltpu.make_async_copy(ref.at[ch, q], ref.at[ch, q], sem.at[ch, q]).wait()
            return 0

        lax.fori_loop(1, 16, one, 0)

    def settle_all():
        for ref, sem in leaving:
            pltpu.make_async_copy(ref, ref, sem).wait()
        leaving.clear()

    def finish(ch):
        def add(d, acc):
            q = (p + d) % 16
            arrived(rs2.at[ch, q], d_r.at[ch, q])
            return acc + rs2[ch, q].astype(F32)

        total = sg[ch, p].astype(F32) + dnb[ch, p].astype(F32)
        out[16 * ch : 16 * ch + 16] = lax.fori_loop(1, 16, add, total).astype(BF)

    attend_groups(0, 1)
    swap()
    attend_groups(1, 2)
    pltpu.make_async_copy(value_up, vup, v_s).wait()
    heads_out(0)
    heads_start(0)
    attend_groups(2, 4)
    heads_mid(0)
    heads_out(1)
    heads_start(1)
    weight(0)
    heads_end(0)
    heads_mid(1)
    project(0, True)
    heads_end(1)
    project(1, False)
    join(0)
    send_proj(1)
    weight(1)
    weight(2)
    expand(0)
    join(1)
    chain(0, 1)
    chain(0, 2)
    expand(1)
    chain(0, 3)
    chain(1, 1)
    activate(0)
    chain(1, 2)
    weight(3)
    lower(0, [kk])
    settle(((ain, a_s), (proj, p_s), (sg, g_s)), (0, 1))
    collect_mid(0)
    chain(1, 3)
    lower(0, [lab(1), lab(-1), lab(2), lab(-2)])
    collect_end(0)
    activate(1)
    lower(0, [lab(3), lab(-3), lab(4)])
    lower(1, [kk])
    settle_all()
    collect_mid(1)
    lower(1, [lab(1), lab(-1), lab(2), lab(-2)])
    settle(((dnb, d_s),), (0,))
    finish(0)
    collect_end(1)
    lower(1, [lab(3), lab(-3), lab(4)])
    settle_all()
    finish(1)
    settle(((dnb, d_s),), (1,))


def layer(lengths, q_latent, q_heads, fresh, cache, value_up, out_proj, residual, gain, gate, up, down):
    vm = pl.BlockSpec(memory_space=pltpu.VMEM)
    hbm = pl.BlockSpec(memory_space=pl.ANY)
    dma = pltpu.SemaphoreType.DMA
    plane = pltpu.VMEM((2, 16, 16, 896), BF)
    return pl.pallas_call(
        layer_kernel,
        out_shape=jax.ShapeDtypeStruct((32, 896), BF),
        in_specs=[pl.BlockSpec(memory_space=pltpu.SMEM), vm, vm, vm, hbm, hbm, hbm, vm, vm, hbm, hbm, hbm],
        out_specs=vm,
        scratch_shapes=[
            pltpu.VMEM((32, 576, 256), BF),
            pltpu.VMEM((16, 512, 128), BF),
            pltpu.VMEM((32, 576), F32),
            pltpu.VMEM((16, 16, 512), F32),
            pltpu.VMEM((2, 2, 16, 1024), BF),
            pltpu.VMEM((2, 512, 896), BF),
            pltpu.VMEM((2, 576, 896), BF),
            pltpu.VMEM((2, 576, 896), BF),
            pltpu.VMEM((2, 576, 896), BF),
            pltpu.VMEM((8, 2, 2, 16, 1024), BF),
            pltpu.VMEM((2, 16, 16, 1024), BF),
            plane, plane, plane, plane,
            pltpu.VMEM((2, 2, 8, 128), F32),
            pltpu.VMEM((2, 8, 8, 128), F32),
            pltpu.VMEM((2, 128, 128), F32),
            pltpu.VMEM((2, 2, 8, 32, 1152), F32),
            pltpu.VMEM((2, 2, 32, 1152), BF),
            pltpu.VMEM((2, 2, 4, 2, 32, 1152), BF),
            pltpu.VMEM((2, 8, 2, 16, 1152), BF),
            plane, plane,
            dma((GROUPS,)), dma,
            dma((4,)), dma((4,)), dma((4,)),
            dma((2, 2, 4, 2)), dma((2, 2, 4, 2)),
            dma((2, 16)), dma((2, 16)),
            dma((2, 16)), dma((2, 16)),
            dma((2, 16)), dma((2, 16)),
            dma((2, 8)), dma((2, 8)),
            dma((2, 2, 4, 2)), dma((2, 2, 4, 2)),
            dma((2, 2, 4, 2)), dma((2, 2, 4, 2)),
            dma((2, 16)), dma((2, 16)),
        ],
        compiler_params=pltpu.CompilerParams(
            collective_id=0, has_side_effects=True, vmem_limit_bytes=53 * 2**20
        ),
        name="layer",
    )(lengths, q_latent, q_heads, fresh, cache, value_up, out_proj, residual, gain, gate, up, down)


def body(
    queries,
    latent_cache,
    fresh_latent_entry,
    lengths,
    key_up_matrix,
    value_up_matrix,
    out_proj,
    residual,
    norm_gain,
    gate_weight,
    up_weight,
    down_weight,
):
    query_heads = queries.reshape(32, 16, 192)
    q_latent = jnp.einsum(
        "rhk,hkl->rhl", query_heads[:, :, :128], key_up_matrix, preferred_element_type=F32
    ).astype(BF)
    return layer(
        lengths,
        q_latent,
        query_heads,
        fresh_latent_entry,
        latent_cache.transpose(0, 2, 1),
        value_up_matrix,
        out_proj,
        residual,
        norm_gain,
        gate_weight.T,
        up_weight.T,
        down_weight,
    )


def solution(mesh):
    return jax.shard_map(
        body,
        mesh=mesh,
        in_specs=(
            P("dp", "tp"),
            P("dp", None, None),
            P("dp", None),
            P("dp"),
            P("tp", None, None),
            P("tp", None, None),
            P("dp", "tp"),
            P("dp", "tp"),
            P("tp"),
            P("tp", "dp"),
            P("tp", "dp"),
            P("dp", "tp"),
        ),
        out_specs=P("dp", "tp"),
        check_vma=False,
    )
```
